32 devices in a mesh: groups: 2 (over x), gx: 8 (over z, y), gy: 2 (over core).
Axes of the slice: x: 2, y: 2, z: 4, core: 2. Of those that a mesh axis runs over, the one named last changes fastest.
Arguments:
- saved_preact: bfloat16 [2048, 49152], P(('groups', 'gy'), 'gx'), parts along dimension 0, may hold values from -6 to 6
- output_grad: bfloat16 [2048, 7424], P(('groups', 'gx'), 'gy'), parts along dimension 0, may hold values from -0.75 to 0.75
- down_weight: bfloat16 [49152, 7424], P('gx', 'gy'), may hold values from -0.5 to 0.5
Outputs:
- preact_grad: bfloat16 [2048, 49152], P(('groups', 'gy'), 'gx'), parts along dimension 0
- weight_grad: bfloat16 [98304, 7424], P(('groups', 'gx'), 'gy'), parts along dimension 0
The draws below stay inside these ranges and needn't reach their ends.
There are 2 independent parts, one for each index of `groups`. The reference program is written for one: setup_inputs(seed, part) draws one part's arguments, and reference() takes and returns one part's arrays. A program takes and returns all parts, laid end to end along the dimension named above; an argument that names none is the same for every part. Nothing has to cross between parts.
All inputs are finite; a program needn't handle non-finite values.
Results may differ from the reference program's by a relative error of at most 0.0051.
Values may be sent and summed in bfloat16 or wider, within the bound.
A program may use at most 256 MiB of HBM per device.

```python
import jax
import jax.numpy as jnp
from jax import lax

D = 7424
FF = 49152
TOK = 1024


def block_scale(key, dims, cuts, least, largest):
    loudness, own = 1.0, jax.random.fold_in(key, 6)
    for axis_at, shards_of in cuts:
        steps = jnp.exp(jax.random.uniform(jax.random.fold_in(own, axis_at), (shards_of,), jnp.float32, least / len(cuts), largest / len(cuts)))
        loudness = loudness * jnp.repeat(steps, dims[axis_at] // shards_of).reshape([-1 if axis == axis_at else 1 for axis in range(len(dims))])
    return loudness


def noise(stream_key, extent, scale, bound, split=(), kind=jnp.bfloat16):
    gain = block_scale(stream_key, extent, split, -0.22, 0.18) if split else 1.0
    result = jax.random.normal(stream_key, extent, jnp.float32) * scale * gain
    return jnp.minimum(jnp.maximum(result, -bound), bound).astype(kind)


def setup_inputs(seed: int = 0, part: int = 0) -> dict:
    arg_keys = jax.random.split(jax.random.key(seed), 4)
    part_splits = jax.random.split(jax.random.fold_in(arg_keys[3], part), 4)
    saved_preact = noise(part_splits[0], (TOK, FF), 1.0, 6.0, ((0, 2), (1, 8)))
    output_grad = noise(part_splits[1], (TOK, D), 0.125, 0.75, ((0, 8), (1, 2)))
    down_weight = noise(arg_keys[2], (FF, D), (D // 64) ** -0.5, 0.5, ((0, 8), (1, 2)))
    return dict(saved_preact=saved_preact, output_grad=output_grad, down_weight=down_weight)


def gelu_value(values):
    return values * 0.5 * (1.0 + jax.scipy.special.erf(values * 0.7071067811865476))


def gelu_slope(values):
    cumulative = 0.5 * (1.0 + jax.scipy.special.erf(values * 0.7071067811865476))
    density = jnp.exp(-0.5 * values * values) * 0.3989422804014327
    return cumulative + values * density


def reference(saved_preact, output_grad, down_weight):
    preact = saved_preact.astype(jnp.float32)
    activation = gelu_value(preact).astype(jnp.bfloat16)
    hidden_grad = lax.dot_general(output_grad, down_weight, (((1,), (1,)), ((), ())), preferred_element_type=jnp.float32)
    preact_grad = (hidden_grad * gelu_slope(preact)).astype(jnp.bfloat16)
    weight_grad = lax.dot_general(activation, output_grad, (((0,), (0,)), ((), ())), preferred_element_type=jnp.float32)
    return preact_grad, weight_grad.astype(jnp.bfloat16)
```

```python
import functools

import jax
import jax.numpy as jnp
from jax import lax
from jax.experimental import pallas as pl
from jax.experimental.pallas import tpu as pltpu
from jax.sharding import PartitionSpec as P

MESH = pl.DeviceIdType.MESH
VMEM_BYTES = 60 * 1024 * 1024
STAGES = 4


def gelu_value(values):
    return values * 0.5 * (1.0 + lax.erf(values * 0.7071067811865476))


def gelu_slope(values):
    cumulative = 0.5 * (1.0 + lax.erf(values * 0.7071067811865476))
    density = jnp.exp(-0.5 * values * values) * 0.3989422804014327
    return cumulative + values * density


def pick_tile(extent):
    return next(tile for tile in (512, 384, 256, 128) if extent % tile == 0)


def gather_kernel(outer, inner, tile, preact, grad, weight, act_out, grad_out, part_own, part_peer,
                  weight_v, grad_v, pre_v, act_v, part_v,
                  weight_sem, own_sem, out_sem, send_sem, recv_sem, pre_sem, act_sem, act_send, act_recv,
                  part_sem, part_send, part_recv):
    me, core = lax.axis_index("gx"), lax.axis_index("gy")
    row, col = me // inner, me % inner
    peer = 1 - core
    shard = grad.shape[0]
    half, hidden = preact.shape
    tiles = hidden // tile
    chunk = shard * inner
    per_half = outer // 2
    up, down = row + 1 < outer, row >= 1
    east, west = col + 1 < inner, col >= 1
    exists = (up, down, east, west)
    target = (me + inner, me - inner, me + 1, me - 1)

    def rows_of(index):
        return pl.ds(pl.multiple_of(index * shard, shard), shard)

    def shard_copy(index, way, src=None):
        place = grad_v.at[rows_of(index)]
        return pltpu.make_async_remote_copy(
            src_ref=place if src is None else src, dst_ref=place,
            send_sem=send_sem.at[way, index], recv_sem=recv_sem.at[index],
            device_id={"gx": target[way]}, device_id_type=MESH)

    def wait_shard(index):
        place = grad_v.at[rows_of(index)]
        pltpu.make_async_remote_copy(
            src_ref=place, dst_ref=place, send_sem=send_sem.at[0, index], recv_sem=recv_sem.at[index],
            device_id={"gx": me}, device_id_type=MESH).wait_recv()

    def send(index, way, src=None):
        @pl.when(exists[way])
        def _():
            shard_copy(index, way, src).start()

    def weight_copy(n):
        rows = pl.ds(pl.multiple_of(n * tile, tile), tile)
        return pltpu.make_async_copy(weight.at[rows], weight_v.at[rows], weight_sem.at[n])

    barrier = pltpu.get_barrier_semaphore()
    for way in range(4):
        @pl.when(exists[way])
        def _():
            pl.semaphore_signal(barrier, inc=1, device_id={"gx": target[way]}, device_id_type=MESH)
    pl.semaphore_signal(barrier, inc=1, device_id={"gy": peer}, device_id_type=MESH)
    count = 1 + sum(jnp.where(e, 1, 0) for e in exists)
    pl.semaphore_wait(barrier, count)

    for way in (2, 3, 0, 1):
        send(me, way, grad)
    own = pltpu.make_async_copy(grad, grad_v.at[rows_of(me)], own_sem)
    own.start()

    def pre_copy(n):
        cols = pl.ds(pl.multiple_of(n * tile, tile), tile)
        return pltpu.make_async_copy(preact.at[:, cols], pre_v.at[n % 2], pre_sem.at[n % 2])

    pre_copy(0).start()

    @pl.loop(0, tiles)
    def _(n):
        weight_copy(n).start()

    own_rows = pl.ds(pl.multiple_of(core * half, half), half)

    def act_copies(n):
        cols = pl.ds(pl.multiple_of(n * tile, tile), tile)
        place = act_out.at[own_rows, cols]
        here = pltpu.make_async_copy(act_v.at[n % 2], place, act_sem.at[n % 2])
        there = pltpu.make_async_remote_copy(
            src_ref=act_v.at[n % 2], dst_ref=place, send_sem=act_send.at[n % 2], recv_sem=act_recv,
            device_id={"gy": peer}, device_id_type=MESH)
        return here, there

    @pl.loop(0, tiles)
    def _(n):
        pre_copy(n).wait()

        @pl.when(n + 1 < tiles)
        def _():
            pre_copy(n + 1).start()

        @pl.when(n >= 2)
        def _():
            here, there = act_copies(n - 2)
            here.wait()
            there.wait_send()

        @pl.loop(0, half // 32)
        def _(s):
            strip = pl.ds(pl.multiple_of(s * 32, 32), 32)
            values = pre_v[n % 2, strip, :].astype(jnp.float32)
            act_v[n % 2, strip, :] = gelu_value(values).astype(jnp.bfloat16)

        here, there = act_copies(n)
        here.start()
        there.start()

    @pl.loop(max(tiles - 2, 0), tiles)
    def _(n):
        here, there = act_copies(n)
        here.wait()
        there.wait_send()

    own.wait()

    near = jnp.minimum(row, outer - 1 - row)

    def chunk_at(k):
        zigzag = jnp.where(k % 2 == 1, row - (k + 1) // 2, row + k // 2)
        rest = jnp.where(row <= outer - 1 - row, k, outer - 1 - k)
        return jnp.where(k <= 2 * near, zigzag, rest)

    def grad_back(c):
        rows = pl.ds(pl.multiple_of(c * chunk, chunk), chunk)
        return pltpu.make_async_copy(grad_v.at[rows], grad_out.at[rows], out_sem.at[c])

    @pl.loop(0, outer)
    def _(k):
        far = k + 1

        @pl.when(row >= far)
        def _():
            index = (row - far) * inner + col
            wait_shard(index)
            send(index, 0)
            send(index, 2)
            send(index, 3)

        @pl.when(row + far < outer)
        def _():
            index = (row + far) * inner + col
            wait_shard(index)
            send(index, 1)
            send(index, 2)
            send(index, 3)

        c = chunk_at(k)

        @pl.loop(1, inner)
        def _(e):
            @pl.when(col >= e)
            def _():
                index = c * inner + col - e
                wait_shard(index)
                send(index, 2)

            @pl.when(col + e < inner)
            def _():
                index = c * inner + col + e
                wait_shard(index)
                send(index, 3)

        grad_back(c).start()
        mine = c // per_half == core
        rows = pl.ds(pl.multiple_of(c * chunk, chunk), chunk)
        part_rows = pl.ds(pl.multiple_of(c % per_half * chunk, chunk), chunk)

        def to_own(n):
            cols = pl.ds(pl.multiple_of(n * tile, tile), tile)
            return pltpu.make_async_copy(
                part_v.at[n % STAGES], part_own.at[part_rows, cols], part_sem.at[n % STAGES])

        def to_peer(n):
            cols = pl.ds(pl.multiple_of(n * tile, tile), tile)
            return pltpu.make_async_remote_copy(
                src_ref=part_v.at[n % STAGES], dst_ref=part_peer.at[part_rows, cols],
                send_sem=part_send.at[n % STAGES], recv_sem=part_recv,
                device_id={"gy": peer}, device_id_type=MESH)

        def drain(n):
            @pl.when(mine)
            def _():
                to_own(n).wait()

            @pl.when(jnp.logical_not(mine))
            def _():
                to_peer(n).wait_send()

        @pl.loop(0, tiles)
        def _(n):
            @pl.when(k == 0)
            def _():
                weight_copy(n).wait()

            @pl.when(n >= STAGES)
            def _():
                drain(n - STAGES)

            part = lax.dot_general(
                grad_v[rows, :], weight_v[pl.ds(pl.multiple_of(n * tile, tile), tile), :],
                (((1,), (1,)), ((), ())), preferred_element_type=jnp.float32)
            part_v[n % STAGES] = part.astype(jnp.bfloat16)

            @pl.when(mine)
            def _():
                to_own(n).start()

            @pl.when(jnp.logical_not(mine))
            def _():
                to_peer(n).start()

        @pl.loop(max(tiles - STAGES, 0), tiles)
        def _(n):
            drain(n)

    @pl.loop(0, outer)
    def _(c):
        grad_back(c).wait()
        line = c * inner + col

        @pl.when(jnp.logical_and(up, c <= row))
        def _():
            shard_copy(line, 0).wait_send()

        @pl.when(jnp.logical_and(down, c >= row))
        def _():
            shard_copy(line, 1).wait_send()

        @pl.loop(0, inner)
        def _(e):
            @pl.when(jnp.logical_and(east, e <= col))
            def _():
                shard_copy(c * inner + e, 2).wait_send()

            @pl.when(jnp.logical_and(west, e >= col))
            def _():
                shard_copy(c * inner + e, 3).wait_send()

    peer_rows = act_out.at[pl.ds(pl.multiple_of(peer * half, half), half)]
    pltpu.make_async_remote_copy(
        src_ref=peer_rows, dst_ref=peer_rows, send_sem=act_send.at[0], recv_sem=act_recv,
        device_id={"gy": peer}, device_id_type=MESH).wait_recv()
    pltpu.make_async_remote_copy(
        src_ref=part_peer, dst_ref=part_peer, send_sem=part_send.at[0], recv_sem=part_recv,
        device_id={"gy": peer}, device_id_type=MESH).wait_recv()


def gather_call(inner, parts, preact, grad, weight):
    half, hidden = preact.shape
    shard, features = grad.shape
    outer = parts // inner
    tile = pick_tile(hidden)
    tokens = shard * parts
    any_spec = pl.BlockSpec(memory_space=pl.ANY)
    return pl.pallas_call(
        functools.partial(gather_kernel, outer, inner, tile),
        out_shape=(
            jax.ShapeDtypeStruct((tokens, hidden), jnp.bfloat16),
            jax.ShapeDtypeStruct((tokens, features), jnp.bfloat16),
            jax.ShapeDtypeStruct((half, hidden), jnp.bfloat16),
            jax.ShapeDtypeStruct((half, hidden), jnp.bfloat16),
        ),
        in_specs=[any_spec] * 3,
        out_specs=(any_spec,) * 4,
        scratch_shapes=[
            pltpu.VMEM((hidden, features), jnp.bfloat16),
            pltpu.VMEM((tokens, features), jnp.bfloat16),
            pltpu.VMEM((2, half, tile), jnp.bfloat16),
            pltpu.VMEM((2, half, tile), jnp.bfloat16),
            pltpu.VMEM((STAGES, shard * inner, tile), jnp.bfloat16),
            pltpu.SemaphoreType.DMA((hidden // tile,)),
            pltpu.SemaphoreType.DMA,
            pltpu.SemaphoreType.DMA((outer,)),
            pltpu.SemaphoreType.DMA((4, parts)),
            pltpu.SemaphoreType.DMA((parts,)),
            pltpu.SemaphoreType.DMA((2,)),
            pltpu.SemaphoreType.DMA((2,)),
            pltpu.SemaphoreType.DMA((2,)),
            pltpu.SemaphoreType.DMA,
            pltpu.SemaphoreType.DMA((STAGES,)),
            pltpu.SemaphoreType.DMA((STAGES,)),
            pltpu.SemaphoreType.DMA,
        ],
        compiler_params=pltpu.CompilerParams(
            collective_id=0, has_side_effects=True, vmem_limit_bytes=VMEM_BYTES),
        cost_estimate=pl.CostEstimate(
            flops=2 * tokens * hidden * features, bytes_accessed=2 * hidden * features,
            transcendentals=half * hidden),
        name="gather_hidden_grad",
    )(preact, grad, weight)


def weight_kernel(act, grad, preact, part_own, part_peer, weight_grad, preact_grad):
    turned = act[...].T
    features = grad.shape[1]
    for start in range(0, features, 1024):
        cols = slice(start, min(start + 1024, features))
        weight_grad[:, cols] = jnp.dot(
            turned, grad[:, cols], preferred_element_type=jnp.float32).astype(jnp.bfloat16)

    @pl.loop(0, preact.shape[0] // 32)
    def _(s):
        strip = pl.ds(pl.multiple_of(s * 32, 32), 32)
        total = part_own[strip, :].astype(jnp.float32) + part_peer[strip, :].astype(jnp.float32)
        slope = gelu_slope(preact[strip, :].astype(jnp.float32))
        preact_grad[strip, :] = (total * slope).astype(jnp.bfloat16)


def weight_call(act, grad, preact, part_own, part_peer):
    tokens, hidden = act.shape
    features = grad.shape[1]
    half = preact.shape[0]
    tile = pick_tile(hidden)
    block = pl.BlockSpec((half, tile), lambda i: (0, i))
    return pl.pallas_call(
        weight_kernel,
        grid=(hidden // tile,),
        out_shape=(
            jax.ShapeDtypeStruct((hidden, features), jnp.bfloat16),
            jax.ShapeDtypeStruct((half, hidden), jnp.bfloat16),
        ),
        in_specs=[
            pl.BlockSpec((tokens, tile), lambda i: (0, i)),
            pl.BlockSpec((tokens, features), lambda i: (0, 0), pipeline_mode=pl.Buffered(1)),
            block, block, block,
        ],
        out_specs=(pl.BlockSpec((tile, features), lambda i: (i, 0)), block),
        compiler_params=pltpu.CompilerParams(vmem_limit_bytes=VMEM_BYTES),
        cost_estimate=pl.CostEstimate(
            flops=2 * tokens * hidden * features, bytes_accessed=2 * hidden * features,
            transcendentals=2 * half * hidden),
        name="weight_grad",
    )(act, grad, preact, part_own, part_peer)


def solution(mesh):
    parts = mesh.shape["gx"]
    inner = 2 ** ((parts.bit_length() - 1) // 2)

    def body(saved_preact, output_grad, down_weight):
        act, grad, part_own, part_peer = gather_call(inner, parts, saved_preact, output_grad, down_weight)
        weight_grad, preact_grad = weight_call(act, grad, saved_preact, part_own, part_peer)
        return preact_grad, weight_grad

    return jax.shard_map(
        body,
        mesh=mesh,
        in_specs=(P(("groups", "gy"), "gx"), P(("groups", "gx"), "gy"), P("gx", "gy")),
        out_specs=(P(("groups", "gy"), "gx"), P(("groups", "gx"), "gy")),
        check_vma=False,
    )
```

```python
import functools

import jax
import jax.numpy as jnp
from jax import lax
from jax.experimental import pallas as pl
from jax.experimental.pallas import tpu as pltpu
from jax.sharding import PartitionSpec as P

MESH = pl.DeviceIdType.MESH
VMEM_BYTES = 60 * 1024 * 1024
STAGES = 2


def pick_tile(extent, most):
    return next(tile for tile in (1024, 768, 512, 384, 256, 128) if tile <= most and extent % tile == 0)


def gather_kernel(outer, inner, tile, small, preact, grad, weight,
                  act_out, slope_out, grad_out, part_own, part_peer,
                  weight_v, grad_v, pre_v, act_v, slope_v, part_v,
                  weight_sem, own_sem, out_sem, send_sem, recv_sem, pre_sem, act_sem, slope_sem, act_send, act_recv,
                  part_sem, part_send, part_recv):
    me, core = lax.axis_index("gx"), lax.axis_index("gy")
    row, col = me // inner, me % inner
    peer = 1 - core
    shard = grad.shape[0]
    half, hidden = preact.shape
    tiles, smalls = hidden // tile, hidden // small
    passes = (pl.ds(0, grad.shape[1]),)
    chunk = shard * inner
    per_half = outer // 2
    up, down = row + 1 < outer, row >= 1
    east, west = col + 1 < inner, col >= 1
    exists = (up, down, east, west)
    target = (me + inner, me - inner, me + 1, me - 1)

    def rows_of(index):
        return pl.ds(pl.multiple_of(index * shard, shard), shard)

    def shard_copy(turn, index, way, own=False):
        place = grad_v.at[rows_of(index), passes[turn]]
        return pltpu.make_async_remote_copy(
            src_ref=grad.at[:, passes[turn]] if own else place, dst_ref=place,
            send_sem=send_sem.at[turn, way, index], recv_sem=recv_sem.at[turn, index],
            device_id={"gx": target[way]}, device_id_type=MESH)

    def wait_shard(turn, index):
        place = grad_v.at[rows_of(index), passes[turn]]
        pltpu.make_async_remote_copy(
            src_ref=place, dst_ref=place, send_sem=send_sem.at[turn, 0, index], recv_sem=recv_sem.at[turn, index],
            device_id={"gx": me}, device_id_type=MESH).wait_recv()

    def send(turn, index, way, own=False):
        @pl.when(exists[way])
        def _():
            shard_copy(turn, index, way, own).start()

    def pass_on(turn, far):
        @pl.when(row >= far)
        def _():
            index = (row - far) * inner + col
            wait_shard(turn, index)
            for way in (0, 2, 3):
                send(turn, index, way)

        @pl.when(row + far < outer)
        def _():
            index = (row + far) * inner + col
            wait_shard(turn, index)
            for way in (1, 2, 3):
                send(turn, index, way)

    def finish_chunk(turn, c):
        @pl.loop(1, inner)
        def _(e):
            @pl.when(col >= e)
            def _():
                index = c * inner + col - e
                wait_shard(turn, index)
                send(turn, index, 2)

            @pl.when(col + e < inner)
            def _():
                index = c * inner + col + e
                wait_shard(turn, index)
                send(turn, index, 3)

    def weight_copy(n):
        rows = pl.ds(pl.multiple_of(n * tile, tile), tile)
        return pltpu.make_async_copy(weight.at[rows], weight_v.at[rows], weight_sem.at[n])

    barrier = pltpu.get_barrier_semaphore()
    for way in range(4):
        @pl.when(exists[way])
        def _():
            pl.semaphore_signal(barrier, inc=1, device_id={"gx": target[way]}, device_id_type=MESH)
    pl.semaphore_signal(barrier, inc=1, device_id={"gy": peer}, device_id_type=MESH)
    count = 1 + sum(jnp.where(e, 1, 0) for e in exists)
    pl.semaphore_wait(barrier, count)

    for way in (2, 3, 0, 1):
        send(0, me, way, True)
    own = pltpu.make_async_copy(grad, grad_v.at[rows_of(me)], own_sem)
    own.start()

    def pre_copy(n):
        cols = pl.ds(pl.multiple_of(n * small, small), small)
        return pltpu.make_async_copy(preact.at[:, cols], pre_v.at[n % 2], pre_sem.at[n % 2])

    pre_copy(0).start()

    own_rows = pl.ds(pl.multiple_of(core * half, half), half)

    def act_copies(n):
        cols = pl.ds(pl.multiple_of(n * small, small), small)
        here = pltpu.make_async_copy(act_v.at[n % 2], act_out.at[own_rows, cols], act_sem.at[n % 2])
        slope = pltpu.make_async_copy(slope_v.at[n % 2], slope_out.at[:, cols], slope_sem.at[n % 2])
        return here, slope

    def act_exchange(n):
        place = act_out.at[own_rows, pl.ds(pl.multiple_of(n * small, small), small)]
        return pltpu.make_async_remote_copy(
            src_ref=place, dst_ref=place, send_sem=act_send.at[n], recv_sem=act_recv.at[n],
            device_id={"gy": peer}, device_id_type=MESH)

    def drain_act(n):
        for copy in act_copies(n):
            copy.wait()
        act_exchange(n).start()

    @pl.loop(0, smalls)
    def _(n):
        pre_copy(n).wait()

        @pl.when(n + 1 < smalls)
        def _():
            pre_copy(n + 1).start()

        @pl.when(n >= 2)
        def _():
            drain_act(n - 2)

        @pl.loop(0, half // 32)
        def _(s):
            strip = pl.ds(pl.multiple_of(s * 32, 32), 32)
            values = pre_v[n % 2, strip, :].astype(jnp.float32)
            cumulative = 0.5 * (1.0 + lax.erf(values * 0.7071067811865476))
            density = jnp.exp(-0.5 * values * values) * 0.3989422804014327
            act_v[n % 2, strip, :] = (values * cumulative).astype(jnp.bfloat16)
            slope_v[n % 2, strip, :] = cumulative + values * density

        for copy in act_copies(n):
            copy.start()

    @pl.loop(max(smalls - 2, 0), smalls)
    def _(n):
        drain_act(n)

    @pl.loop(0, tiles)
    def _(n):
        weight_copy(n).start()

    own.wait()

    near = jnp.minimum(row, outer - 1 - row)

    def chunk_at(k):
        zigzag = jnp.where(k % 2 == 1, row - (k + 1) // 2, row + k // 2)
        rest = jnp.where(row <= outer - 1 - row, k, outer - 1 - k)
        return jnp.where(k <= 2 * near, zigzag, rest)

    def grad_back(c):
        rows = pl.ds(pl.multiple_of(c * chunk, chunk), chunk)
        return pltpu.make_async_copy(grad_v.at[rows], grad_out.at[rows], out_sem.at[c])

    def part_place(k, n):
        c = chunk_at(k)
        rows = pl.ds(pl.multiple_of(c % per_half * chunk, chunk), chunk)
        return c // per_half == core, rows, pl.ds(pl.multiple_of(n * tile, tile), tile)

    def to_own(step, rows, cols):
        slot = step % STAGES
        return pltpu.make_async_copy(part_v.at[slot], part_own.at[rows, cols], part_sem.at[slot])

    def to_peer(step, rows, cols):
        slot = step % STAGES
        return pltpu.make_async_remote_copy(
            src_ref=part_v.at[slot], dst_ref=part_peer.at[rows, cols],
            send_sem=part_send.at[slot], recv_sem=part_recv,
            device_id={"gy": peer}, device_id_type=MESH)

    def drain(step):
        mine, rows, cols = part_place(step // tiles, step % tiles)

        @pl.when(mine)
        def _():
            to_own(step, rows, cols).wait()

        @pl.when(jnp.logical_not(mine))
        def _():
            to_peer(step, rows, cols).wait_send()

    @pl.loop(0, outer)
    def _(k):
        pass_on(0, k + 1)
        c = chunk_at(k)
        finish_chunk(0, c)
        grad_back(c).start()
        token_rows = pl.ds(pl.multiple_of(c * chunk, chunk), chunk)

        @pl.loop(0, tiles)
        def _(n):
            step = k * tiles + n

            @pl.when(k == 0)
            def _():
                weight_copy(n).wait()

            @pl.when(step >= STAGES)
            def _():
                drain(step - STAGES)

            part = lax.dot_general(
                grad_v[token_rows, :], weight_v[pl.ds(pl.multiple_of(n * tile, tile), tile), :],
                (((1,), (1,)), ((), ())), preferred_element_type=jnp.float32)
            part_v[step % STAGES] = part.astype(jnp.bfloat16)
            mine, rows, cols = part_place(k, n)

            @pl.when(mine)
            def _():
                to_own(step, rows, cols).start()

            @pl.when(jnp.logical_not(mine))
            def _():
                to_peer(step, rows, cols).start()

    @pl.loop(outer * tiles - STAGES, outer * tiles)
    def _(step):
        drain(step)

    @pl.loop(0, smalls)
    def _(n):
        act_exchange(n).wait()

    @pl.loop(0, outer)
    def _(c):
        grad_back(c).wait()
        line = c * inner + col

        for turn in range(1):
            @pl.when(jnp.logical_and(up, c <= row))
            def _():
                shard_copy(turn, line, 0).wait_send()

            @pl.when(jnp.logical_and(down, c >= row))
            def _():
                shard_copy(turn, line, 1).wait_send()

            @pl.loop(0, inner)
            def _(e):
                @pl.when(jnp.logical_and(east, e <= col))
                def _():
                    shard_copy(turn, c * inner + e, 2).wait_send()

                @pl.when(jnp.logical_and(west, e >= col))
                def _():
                    shard_copy(turn, c * inner + e, 3).wait_send()

    pltpu.make_async_remote_copy(
        src_ref=part_peer, dst_ref=part_peer, send_sem=part_send.at[0], recv_sem=part_recv,
        device_id={"gy": peer}, device_id_type=MESH).wait_recv()


def gather_call(inner, parts, preact, grad, weight):
    half, hidden = preact.shape
    shard, features = grad.shape
    outer = parts // inner
    tile, small = pick_tile(hidden, 1024), pick_tile(hidden, 256)
    tokens = shard * parts
    any_spec = pl.BlockSpec(memory_space=pl.ANY)
    return pl.pallas_call(
        functools.partial(gather_kernel, outer, inner, tile, small),
        out_shape=(
            jax.ShapeDtypeStruct((tokens, hidden), jnp.bfloat16),
            jax.ShapeDtypeStruct((half, hidden), jnp.float32),
            jax.ShapeDtypeStruct((tokens, features), jnp.bfloat16),
            jax.ShapeDtypeStruct((half, hidden), jnp.bfloat16),
            jax.ShapeDtypeStruct((half, hidden), jnp.bfloat16),
        ),
        in_specs=[any_spec] * 3,
        out_specs=(any_spec,) * 5,
        scratch_shapes=[
            pltpu.VMEM((hidden, features), jnp.bfloat16),
            pltpu.VMEM((tokens, features), jnp.bfloat16),
            pltpu.VMEM((2, half, small), jnp.bfloat16),
            pltpu.VMEM((2, half, small), jnp.bfloat16),
            pltpu.VMEM((2, half, small), jnp.float32),
            pltpu.VMEM((STAGES, shard * inner, tile), jnp.bfloat16),
            pltpu.SemaphoreType.DMA((hidden // tile,)),
            pltpu.SemaphoreType.DMA,
            pltpu.SemaphoreType.DMA((outer,)),
            pltpu.SemaphoreType.DMA((1, 4, parts)),
            pltpu.SemaphoreType.DMA((1, parts)),
            pltpu.SemaphoreType.DMA((2,)),
            pltpu.SemaphoreType.DMA((2,)),
            pltpu.SemaphoreType.DMA((2,)),
            pltpu.SemaphoreType.DMA((hidden // small,)),
            pltpu.SemaphoreType.DMA((hidden // small,)),
            pltpu.SemaphoreType.DMA((STAGES,)),
            pltpu.SemaphoreType.DMA((STAGES,)),
            pltpu.SemaphoreType.DMA,
        ],
        compiler_params=pltpu.CompilerParams(
            collective_id=0, has_side_effects=True, vmem_limit_bytes=VMEM_BYTES),
        cost_estimate=pl.CostEstimate(
            flops=2 * tokens * hidden * features, bytes_accessed=2 * hidden * features,
            transcendentals=half * hidden),
        name="gather_hidden_grad",
    )(preact, grad, weight)


def weight_kernel(act, grad, slope, part_own, part_peer, weight_grad, preact_grad):
    turned = act[...].T
    rest = grad.shape[1]
    for start in range(0, rest, 1024):
        stop = min(start + 1024, rest)
        weight_grad[:, start:stop] = jnp.dot(
            turned, grad[:, start:stop], preferred_element_type=jnp.float32).astype(jnp.bfloat16)
    for start in range(0, slope.shape[0], 32):
        strip = slice(start, start + 32)
        total = part_own[strip, :].astype(jnp.float32) + part_peer[strip, :].astype(jnp.float32)
        preact_grad[strip, :] = (total * slope[strip, :]).astype(jnp.bfloat16)


def weight_call(act, slope, grad, part_own, part_peer):
    tokens, hidden = act.shape
    features = grad.shape[1]
    half = slope.shape[0]
    tile = pick_tile(hidden, 512)
    block = pl.BlockSpec((half, tile), lambda i: (0, i))
    return pl.pallas_call(
        weight_kernel,
        grid=(hidden // tile,),
        out_shape=(
            jax.ShapeDtypeStruct((hidden, features), jnp.bfloat16),
            jax.ShapeDtypeStruct((half, hidden), jnp.bfloat16),
        ),
        in_specs=[
            pl.BlockSpec((tokens, tile), lambda i: (0, i)),
            pl.BlockSpec((tokens, features), lambda i: (0, 0), pipeline_mode=pl.Buffered(1)),
            block, block, block,
        ],
        out_specs=(pl.BlockSpec((tile, features), lambda i: (i, 0)), block),
        compiler_params=pltpu.CompilerParams(vmem_limit_bytes=VMEM_BYTES),
        cost_estimate=pl.CostEstimate(
            flops=2 * tokens * hidden * features, bytes_accessed=4 * hidden * features, transcendentals=0),
        name="weight_grad",
    )(act, grad, slope, part_own, part_peer)


def solution(mesh):
    parts = mesh.shape["gx"]
    inner = 2 ** ((parts.bit_length() - 1) // 2)

    def body(saved_preact, output_grad, down_weight):
        act, slope, grad, part_own, part_peer = gather_call(
            inner, parts, saved_preact, output_grad, down_weight)
        weight_grad, preact_grad = weight_call(act, slope, grad, part_own, part_peer)
        return preact_grad, weight_grad

    return jax.shard_map(
        body,
        mesh=mesh,
        in_specs=(P(("groups", "gy"), "gx"), P(("groups", "gx"), "gy"), P("gx", "gy")),
        out_specs=(P(("groups", "gy"), "gx"), P(("groups", "gx"), "gy")),
        check_vma=False,
    )
```
